32 devices in a mesh: agg: 4 (over y, core), blk: 8 (over z, x).
Axes of the slice: x: 2, y: 2, z: 4, core: 2. Of those that a mesh axis runs over, the one named last changes fastest.
Arguments:
- right_side: float32 [128, 256, 128], P('blk', 'agg'), may hold values from -8 to 8
- coefficient: float32 [128, 256, 128], P('blk', 'agg'), may hold values from 0.05 to 2
Outputs:
- pressure: float32 [128, 256, 128], P('blk', 'agg')
The draws below stay inside these ranges and needn't reach their ends.
All inputs are finite; a program needn't handle non-finite values.
Results may differ from the reference program's by a relative error of at most 0.0001.
Values sent between devices are 32-bit elements; how exact they have to be, the bound alone decides.
A program may use at most 128 MiB of HBM per device.

```python
import math
import jax
import jax.numpy as jnp

CY = 64
LEVELS = 2
NX = 128
NY = 256
NZ = 128


def block_scale(own_key, shape, split, smallest, top_value):
    gain = 1.0
    for axis_at, blocks in split:
        steps = jax.random.uniform(jax.random.fold_in(jax.random.fold_in(own_key, 6), axis_at), (blocks,), jnp.float32, smallest / len(split), top_value / len(split))
        gain = gain * jnp.repeat(jnp.exp(steps), shape[axis_at] // blocks).reshape((-1,) + (1,) * (len(shape) - 1 - axis_at))
    return gain


def scatter_about(rng, dims, deviation, most, pieces=(), kind=jnp.bfloat16):
    drawn = jax.random.normal(rng, dims, jnp.float32) * deviation
    if len(pieces) > 0:
        drawn = block_scale(rng, dims, pieces, -0.22, 0.18) * drawn
    return jnp.clip(drawn, min=-most, max=most).astype(kind)


def setup_inputs(seed: int = 0) -> dict:
    key_list = jax.random.split(jax.random.key(seed), 3)
    return {
        "right_side": scatter_about(key_list[0], (NX, NY, NZ), 1.0, 8.0, ((0, 8), (1, 4)), jnp.float32),
        "coefficient": jnp.clip(jnp.exp(math.log(2.0) - 3.6888794 * jax.random.uniform(key_list[1], (NX, NY, NZ), jnp.float32) ** block_scale(key_list[1], (NX, NY, NZ), ((0, 8), (1, 4)), -0.2, 0.2)), 0.05, 2.0),
    }


OMEGA = 0.8


def neighbours(v, window):
    nx, ny, nz = v.shape
    p = jnp.pad(v, ((1, 1), (0, 0), (1, 1)))
    total = p[2:, :, 1:-1] + p[:-2, :, 1:-1] + p[1:-1, :, 2:] + p[1:-1, :, :-2]
    if window == 0:
        q = jnp.pad(v, ((0, 0), (1, 1), (0, 0)))
        total = total + q[:, 2:] + q[:, :-2]
    else:
        w = v.reshape(nx, ny // window, window, nz)
        q = jnp.pad(w, ((0, 0), (0, 0), (1, 1), (0, 0)))
        total = total + (q[:, :, 2:] + q[:, :, :-2]).reshape(nx, ny, nz)
    return total


def operate(v, coef, window):
    return (6.0 + coef) * v - neighbours(v, window)


def smooth(v, rhs, coef, window):
    return v + OMEGA * (rhs - operate(v, coef, window)) / (6.0 + coef)


def restrict(v):
    nx, ny, nz = v.shape
    return v.reshape(nx // 2, 2, ny // 2, 2, nz // 2, 2).sum(axis=(1, 3, 5)) * 0.5


def prolong(v):
    return jnp.repeat(jnp.repeat(jnp.repeat(v, 2, axis=0), 2, axis=1), 2, axis=2)


def reference(right_side, coefficient):
    fine = OMEGA * right_side / (6.0 + coefficient)
    fine = smooth(fine, right_side, coefficient, 0)
    resid = right_side - operate(fine, coefficient, 0)
    rhs_list = [right_side]
    coef_list = [coefficient]
    err_list = [fine]
    for level in range(1, LEVELS + 1):
        target = restrict(resid)
        coef = restrict(coef_list[-1])
        err = OMEGA * target / (6.0 + coef)
        if level == LEVELS:
            err = smooth(err, target, coef, CY)
        else:
            resid = target - operate(err, coef, CY)
        rhs_list.append(target)
        coef_list.append(coef)
        err_list.append(err)
    for level in range(LEVELS, 0, -1):
        window = CY if level > 1 else 0
        merged = err_list[level - 1] + prolong(err_list[level])
        err_list[level - 1] = smooth(merged, rhs_list[level - 1], coef_list[level - 1], window)
    return err_list[0]
```

```python
import functools

import jax
import jax.numpy as jnp
from jax import lax
from jax.experimental import pallas as pl
from jax.experimental.pallas import tpu as pltpu
from jax.sharding import PartitionSpec as P

OMEGA = 0.8
WIDE = 2
EDGE = 8
TOP = 16

SIDES = [(dx, dy) for dx in (-1, 0, 1) for dy in (-1, 0, 1) if (dx, dy) != (0, 0)]


def padded_shape(nx, ny, nz):
    return (nx + 2 * WIDE, ny + 2 * TOP, nz)


def depth_pair(field, step):
    axis = field.ndim - 1
    depth = field.shape[axis]
    column = lax.broadcasted_iota(jnp.int32, field.shape, axis)
    ahead = jnp.where(column < depth - step, pltpu.roll(field, depth - step, axis), 0.0)
    behind = jnp.where(column >= step, pltpu.roll(field, step, axis), 0.0)
    return ahead + behind


def depth_sum(field, step):
    axis = field.ndim - 1
    depth = field.shape[axis]
    column = lax.broadcasted_iota(jnp.int32, field.shape, axis)
    ahead = pltpu.roll(field, depth - step, axis)
    behind = pltpu.roll(field, step, axis)
    return field + jnp.where((column // step) % 2 == 0, ahead, behind)


def around(ref, i, first, count, step, cut=None):
    rows = pl.ds(first, count)
    own = ref[i, rows]
    up = ref[i, pl.ds(first - 1, count)]
    down = ref[i, pl.ds(first + 1, count)]
    if cut is not None:
        up = up * cut[0]
        down = down * cut[1]
    total = ref[i - 1, rows] + ref[i + 1, rows] + (up + down)
    return own, total + depth_pair(own, step)


def loop(low, high, body, unroll=2):
    def step(i, carry):
        body(i)
        return carry

    lax.fori_loop(low, high, step, 0, unroll=unroll)


def halo_copies(ref, nx, ny, planes, corners, sems, base):
    copies = []
    blk, agg = lax.axis_index("blk"), lax.axis_index("agg")
    for dx, dy in SIDES:
        if dx != 0 and dy != 0 and not corners:
            continue
        x_from, x_to, x_count = {
            -1: (WIDE, nx + WIDE, planes),
            0: (WIDE, WIDE, nx),
            1: (nx + WIDE - planes, WIDE - planes, planes),
        }[dx]
        y_from, y_to, y_count = {
            -1: (TOP, TOP + ny, EDGE),
            0: (TOP, TOP, ny),
            1: (TOP + ny - EDGE, TOP - EDGE, EDGE),
        }[dy]
        at = base + len(copies)
        copy = pltpu.make_async_remote_copy(
            src_ref=ref.at[pl.ds(x_from, x_count), pl.ds(y_from, y_count)],
            dst_ref=ref.at[pl.ds(x_to, x_count), pl.ds(y_to, y_count)],
            send_sem=sems[0].at[at],
            recv_sem=sems[1].at[at],
            device_id={"blk": blk + dx, "agg": agg + dy},
            device_id_type=pl.DeviceIdType.MESH,
        )
        copies.append(((dx, dy), copy))
    return copies


def kernel(levels, *refs):
    refs = list(refs)
    rhs_ref, coef_ref, out_ref = refs[:3]
    refs = refs[3:]
    take = lambda count: [refs.pop(0) for _ in range(count)]
    vs = take(levels + 1)
    ws = take(levels + 1)
    ps = take(levels + 1)
    bs = take(levels + 1)
    cs = take(levels + 1)
    ts = take(levels)
    us = take(levels)
    sems = take(2)

    nx, ny, nz = rhs_ref.shape
    shapes = [(nx >> k, ny >> k, nz) for k in range(levels + 1)]
    blk, agg = lax.axis_index("blk"), lax.axis_index("agg")
    n_blk, n_agg = lax.axis_size("blk"), lax.axis_size("agg")

    def inside(dx, dy):
        ok = None
        for d, at, size in ((dx, blk, n_blk), (dy, agg, n_agg)):
            if d == 0:
                continue
            this = at > 0 if d < 0 else at < size - 1
            ok = this if ok is None else jnp.logical_and(ok, this)
        return ok

    barrier = pltpu.get_barrier_semaphore()
    for dx, dy in SIDES:

        @pl.when(inside(dx, dy))
        def _():
            pl.semaphore_signal(
                barrier,
                inc=1,
                device_id={"blk": blk + dx, "agg": agg + dy},
                device_id_type=pl.DeviceIdType.MESH,
            )

    @pl.when(blk == 0)
    def _():
        for ref in vs + ws:
            ref[0:WIDE] = jnp.zeros((WIDE,) + ref.shape[1:], jnp.float32)

    @pl.when(blk == n_blk - 1)
    def _():
        for ref in vs + ws:
            high = ref.shape[0]
            ref[high - WIDE : high] = jnp.zeros((WIDE,) + ref.shape[1:], jnp.float32)

    @pl.when(agg == 0)
    def _():
        for ref in vs + ws:
            zero = jnp.zeros((ref.shape[0], EDGE, nz), jnp.float32)
            ref[:, TOP - EDGE : TOP] = zero

    @pl.when(agg == n_agg - 1)
    def _():
        for ref in vs + ws:
            high = ref.shape[1] - TOP
            zero = jnp.zeros((ref.shape[0], EDGE, nz), jnp.float32)
            ref[:, high : high + EDGE] = zero

    own_rows = pl.ds(TOP, ny)

    def guess(i):
        scale = OMEGA / (6.0 + coef_ref[i])
        ws[0][i + WIDE, own_rows] = scale
        vs[0][i + WIDE, own_rows] = scale * rhs_ref[i]

    loop(0, nx, guess)

    count = 1
    for size, at in ((n_blk, blk), (n_agg, agg)):
        near = 1 + (at > 0).astype(jnp.int32) + (at < size - 1).astype(jnp.int32)
        count = count * near
    pl.semaphore_wait(barrier, count - 1)

    pending = []
    used = [0]

    def send(ref, k, planes, corners):
        copies = halo_copies(ref, *shapes[k][:2], planes, corners, sems, used[0])
        used[0] += len(copies)
        for (dx, dy), copy in copies:

            @pl.when(inside(dx, dy))
            def _():
                copy.start()

        pending.extend(copies)
        return copies

    def receive(copies):
        for (dx, dy), copy in copies:

            @pl.when(inside(-dx, -dy))
            def _():
                copy.wait_recv()

    def coarsened(source, k, i):
        rows = shapes[k][1]
        held = ts[k - 1]
        held[i] = source
        pair = held[i, pl.ds(0, rows, stride=2)] + held[i, pl.ds(1, rows, stride=2)]
        return 0.5 * depth_sum(pair, 1 << (k - 1))

    v_moves = [send(vs[0], 0, WIDE, True)]
    w_moves = [send(ws[0], 0, 1, False)]

    for k in range(1, levels + 1):
        above = coef_ref if k == 1 else cs[k - 1]

        def scales(i, k=k, above=above):
            coef = coarsened(above[2 * i] + above[2 * i + 1], k, i)
            cs[k][i] = coef
            ws[k][i + WIDE, pl.ds(TOP, shapes[k][1])] = OMEGA / (6.0 + coef)

        loop(0, shapes[k][0], scales)
        w_moves.append(send(ws[k], k, 1, k > 1))

    receive(v_moves[0])
    receive(w_moves[0])

    def smooth_fine(i):
        own, total = around(vs[0], i, TOP - EDGE, ny + 2 * EDGE, 1)
        ps[0][i, pl.ds(TOP - EDGE, ny + 2 * EDGE)] = (
            1.2 * own + ws[0][i, pl.ds(TOP - EDGE, ny + 2 * EDGE)] * total
        )
        return total[EDGE : EDGE + ny]

    def smooth_own(i):
        total = smooth_fine(i + WIDE)
        bs[0][i] = 0.04 * rhs_ref[i] - OMEGA * total

    smooth_fine(WIDE - 1)
    loop(0, nx, smooth_own)
    smooth_fine(nx + WIDE)

    def fine_residual(i):
        _, total = around(ps[0], i + WIDE, TOP, ny, 1)
        return bs[0][i] + total

    def cuts(k, first, rows):
        span = 1 << k
        low = (agg % span != 0).astype(jnp.float32)
        high = ((agg + 1) % span != 0).astype(jnp.float32)
        row = first + lax.broadcasted_iota(jnp.int32, (rows, nz), 0)
        end = TOP + shapes[k][1]
        up = jnp.where(row == TOP, low, jnp.where(row == end, high, 1.0))
        down = jnp.where(row == TOP - 1, low, jnp.where(row == end - 1, high, 1.0))
        return up, down

    for k in range(1, levels + 1):
        kx, ky, _ = shapes[k]
        if k == 1:
            residual = fine_residual
        else:
            cut = cuts(k - 1, TOP, shapes[k - 1][1])

            def residual(i, k=k, cut=cut):
                _, total = around(
                    vs[k - 1], i + WIDE, TOP, shapes[k - 1][1], 1 << (k - 1), cut
                )
                return 0.2 * bs[k - 1][i] + total

        def descend(i, k=k, residual=residual):
            source = coarsened(residual(2 * i) + residual(2 * i + 1), k, i)
            bs[k][i] = source
            rows = pl.ds(TOP, shapes[k][1])
            vs[k][i + WIDE, rows] = ws[k][i + WIDE, rows] * source

        loop(0, kx, descend)
        v_moves.append(send(vs[k], k, WIDE, True))
        receive(v_moves[k])

    for k in range(1, levels + 1):
        receive(w_moves[k])

    def spread(k, i):
        count = shapes[k + 1][1] + EDGE
        coarse = cs_error[k + 1][i, pl.ds(TOP - EDGE // 2, count)]
        us[k][i, pl.ds(TOP - EDGE, count, stride=2)] = coarse
        us[k][i, pl.ds(TOP - EDGE + 1, count, stride=2)] = coarse
        return us[k][i, pl.ds(TOP - EDGE, 2 * count)]

    cs_error = es = [None] + take(levels)

    for k in range(levels, 0, -1):
        kx, ky, _ = shapes[k]
        rows = pl.ds(TOP - EDGE, ky + 2 * EDGE)
        cut = cuts(k, TOP - EDGE, ky + 2 * EDGE)
        if k == levels:

            def relax(i, k=k, rows=rows, cut=cut, ky=ky):
                own, total = around(vs[k], i, TOP - EDGE, ky + 2 * EDGE, 1 << k, cut)
                es[k][i, rows] = 1.2 * own + ws[k][i, rows] * total
        else:

            def merge(i, k=k, rows=rows):
                extra = spread(k, i)
                for j in range(2):
                    at = 2 * (i - 1) + j
                    ps[k][at, rows] = vs[k][at, rows] + extra

            loop(1, shapes[k + 1][0] + WIDE + 1, merge)

            def relax(i, k=k, rows=rows, cut=cut, ky=ky):
                own, total = around(ps[k], i, TOP - EDGE, ky + 2 * EDGE, 1 << k, cut)
                es[k][i, rows] = 0.2 * own + (vs[k][i, rows] + ws[k][i, rows] * total)

        loop(1, kx + WIDE + 1, relax)

    def merge_fine(i):
        extra = spread(0, i)
        rows = pl.ds(TOP - EDGE, ny + 2 * EDGE)
        for j in range(2):
            at = 2 * (i - 1) + j
            ps[0][at, rows] = ps[0][at, rows] + extra

    loop(1, shapes[1][0] + WIDE + 1, merge_fine)

    def finish(i):
        own, total = around(ps[0], i + WIDE, TOP, ny, 1)
        at = i + WIDE
        out_ref[i] = 0.2 * own + (vs[0][at, own_rows] + ws[0][at, own_rows] * total)

    loop(0, nx, finish)

    for (dx, dy), copy in pending:

        @pl.when(inside(dx, dy))
        def _():
            copy.wait_send()


def shards(right_side, coefficient):
    levels = lax.axis_size("agg").bit_length() - 1
    nx, ny, nz = right_side.shape
    shapes = [(nx >> k, ny >> k, nz) for k in range(levels + 1)]
    vmem = lambda shape: pltpu.VMEM(shape, jnp.float32)
    padded = [vmem(padded_shape(*shape)) for shape in shapes]
    plain = [vmem(shape) for shape in shapes]
    halves = [vmem((shapes[k + 1][0], shapes[k][1], nz)) for k in range(levels)]
    spreads = [
        vmem((shapes[k + 1][0] + 2 * WIDE, shapes[k][1] + 2 * TOP, nz)) for k in range(levels)
    ]
    moves = 16 * (levels + 1)
    sems = [pltpu.SemaphoreType.DMA((moves,))] * 2
    cells = nx * ny * nz
    return pl.pallas_call(
        functools.partial(kernel, levels),
        out_shape=jax.ShapeDtypeStruct(right_side.shape, right_side.dtype),
        in_specs=[pl.BlockSpec(memory_space=pltpu.VMEM)] * 2,
        out_specs=pl.BlockSpec(memory_space=pltpu.VMEM),
        scratch_shapes=padded * 3 + plain * 2 + halves + spreads + sems + padded[1:],
        compiler_params=pltpu.CompilerParams(
            collective_id=0, has_side_effects=True, vmem_limit_bytes=40 * 2**20
        ),
        cost_estimate=pl.CostEstimate(
            flops=60 * cells, bytes_accessed=12 * cells, transcendentals=0
        ),
        name="vcycle",
    )(right_side, coefficient)


def solution(mesh):
    placed = (P("blk", "agg", None), P("blk", "agg", None))
    return jax.shard_map(
        shards, mesh=mesh, in_specs=placed, out_specs=P("blk", "agg", None), check_vma=False
    )
```

```python
import functools

import jax
import jax.numpy as jnp
from jax import lax
from jax.experimental import pallas as pl
from jax.experimental.pallas import tpu as pltpu
from jax.sharding import PartitionSpec as P

OMEGA = 0.8
WIDE = 2
EDGE = 8
TOP = 16

SIDES = [(dx, dy) for dx in (-1, 0, 1) for dy in (-1, 0, 1) if (dx, dy) != (0, 0)]


def padded_shape(nx, ny, nz):
    return (nx + 2 * WIDE, ny + 2 * TOP, nz)


def depth_pair(field, step):
    axis = field.ndim - 1
    depth = field.shape[axis]
    column = lax.broadcasted_iota(jnp.int32, field.shape, axis)
    ahead = jnp.where(column < depth - step, pltpu.roll(field, depth - step, axis), 0.0)
    behind = jnp.where(column >= step, pltpu.roll(field, step, axis), 0.0)
    return ahead + behind


def depth_sum(field, step):
    axis = field.ndim - 1
    depth = field.shape[axis]
    column = lax.broadcasted_iota(jnp.int32, field.shape, axis)
    ahead = pltpu.roll(field, depth - step, axis)
    behind = pltpu.roll(field, step, axis)
    return field + jnp.where((column // step) % 2 == 0, ahead, behind)


def around(ref, i, first, count, step, cut=None):
    rows = pl.ds(first, count)
    own = ref[i, rows]
    up = ref[i, pl.ds(first - 1, count)]
    down = ref[i, pl.ds(first + 1, count)]
    if cut is not None:
        up = up * cut[0]
        down = down * cut[1]
    total = ref[i - 1, rows] + ref[i + 1, rows] + (up + down)
    return own, total + depth_pair(own, step)


UNROLL = 4


def loop(low, high, body, unroll=UNROLL):
    trips = high - low
    if trips <= unroll:
        for i in range(low, high):
            body(i)
        return
    while trips % unroll:
        unroll -= 1

    def step(i, carry):
        for j in range(unroll):
            body(low + i * unroll + j)
        return carry

    lax.fori_loop(0, trips // unroll, step, 0)


X_FACES = [(-1, 0), (1, 0)]
Y_FACES = [(0, -1), (0, 1)]
CORNERS = [(-1, -1), (-1, 1), (1, -1), (1, 1)]


def halo_copies(ref, nx, ny, planes, corners, sems, base):
    copies = {}
    blk, agg = lax.axis_index("blk"), lax.axis_index("agg")
    for dx, dy in SIDES:
        if dx != 0 and dy != 0 and not corners:
            continue
        x_from, x_to, x_count = {
            -1: (WIDE, nx + WIDE, planes),
            0: (WIDE, WIDE, nx),
            1: (nx + WIDE - planes, WIDE - planes, planes),
        }[dx]
        y_from, y_to, y_count = {
            -1: (TOP, TOP + ny, EDGE),
            0: (TOP, TOP, ny),
            1: (TOP + ny - EDGE, TOP - EDGE, EDGE),
        }[dy]
        at = base + len(copies)
        copy = pltpu.make_async_remote_copy(
            src_ref=ref.at[pl.ds(x_from, x_count), pl.ds(y_from, y_count)],
            dst_ref=ref.at[pl.ds(x_to, x_count), pl.ds(y_to, y_count)],
            send_sem=sems[0].at[at],
            recv_sem=sems[1].at[at],
            device_id={"blk": blk + dx, "agg": agg + dy},
            device_id_type=pl.DeviceIdType.MESH,
        )
        copies[dx, dy] = copy
    return copies


def kernel(levels, *refs):
    refs = list(refs)
    rhs_hbm, coef_hbm, out_hbm = refs[:3]
    refs = refs[3:]
    take = lambda count: [refs.pop(0) for _ in range(count)]
    vs = take(levels + 1)
    ws = take(levels + 1)
    fs = take(levels + 1)
    bs = take(levels + 1)
    cs = take(levels + 1)
    ts = take(levels)
    us = take(levels)
    ps, rhs_ref = take(2)
    coef_ref = cs[0]
    send_sem, recv_sem, load_sem, store_sem = take(4)
    out_ref = rhs_ref

    nx, ny, nz = rhs_ref.shape
    shapes = [(nx >> k, ny >> k, nz) for k in range(levels + 1)]
    blk, agg = lax.axis_index("blk"), lax.axis_index("agg")
    n_blk, n_agg = lax.axis_size("blk"), lax.axis_size("agg")

    part = nx // 4
    loads = {}
    for at, q in enumerate((0, 3, 1, 2)):
        planes = pl.ds(q * part, part)
        loads[q] = [
            pltpu.make_async_copy(hbm.at[planes], ref.at[planes], load_sem.at[2 * at + j])
            for j, (hbm, ref) in enumerate(((coef_hbm, coef_ref), (rhs_hbm, rhs_ref)))
        ]
        for copy in loads[q]:
            copy.start()

    def inside(dx, dy):
        ok = None
        for d, at, size in ((dx, blk, n_blk), (dy, agg, n_agg)):
            if d == 0:
                continue
            this = at > 0 if d < 0 else at < size - 1
            ok = this if ok is None else jnp.logical_and(ok, this)
        return ok

    barrier = pltpu.get_barrier_semaphore()
    for dx, dy in SIDES:

        @pl.when(inside(dx, dy))
        def _():
            pl.semaphore_signal(
                barrier,
                inc=1,
                device_id={"blk": blk + dx, "agg": agg + dy},
                device_id_type=pl.DeviceIdType.MESH,
            )

    @pl.when(blk == 0)
    def _():
        for ref in vs + ws:
            ref[0:WIDE] = jnp.zeros((WIDE,) + ref.shape[1:], jnp.float32)

    @pl.when(blk == n_blk - 1)
    def _():
        for ref in vs + ws:
            high = ref.shape[0]
            ref[high - WIDE : high] = jnp.zeros((WIDE,) + ref.shape[1:], jnp.float32)

    @pl.when(agg == 0)
    def _():
        for ref in vs + ws:
            zero = jnp.zeros((ref.shape[0], EDGE, nz), jnp.float32)
            ref[:, TOP - EDGE : TOP] = zero

    @pl.when(agg == n_agg - 1)
    def _():
        for ref in vs + ws:
            high = ref.shape[1] - TOP
            zero = jnp.zeros((ref.shape[0], EDGE, nz), jnp.float32)
            ref[:, high : high + EDGE] = zero

    used = 0
    v_moves, w_moves = [], []
    for k in range(levels + 1):
        for ref, moves, planes, corners in (
            (vs[k], v_moves, WIDE, True),
            (ws[k], w_moves, 1, k > 1),
        ):
            copies = halo_copies(
                ref, *shapes[k][:2], planes, corners, (send_sem, recv_sem), used
            )
            moves.append(copies)
            used += len(copies)

    def send(copies, sides):
        for dx, dy in sides:

            @pl.when(inside(dx, dy))
            def _():
                copies[dx, dy].start()

    def receive(copies, sides):
        for dx, dy in sides:

            @pl.when(inside(-dx, -dy))
            def _():
                copies[dx, dy].wait_recv()

    own_rows = pl.ds(TOP, ny)

    def guess(i):
        scale = OMEGA / (6.0 + coef_ref[i])
        ws[0][i + WIDE, own_rows] = scale
        vs[0][i + WIDE, own_rows] = scale * rhs_ref[i]

    def guess_part(q):
        for copy in loads[q]:
            copy.wait()
        loop(q * part, (q + 1) * part, guess)

    guess_part(0)
    guess_part(3)
    count = 1
    for size, at in ((n_blk, blk), (n_agg, agg)):
        near = 1 + (at > 0).astype(jnp.int32) + (at < size - 1).astype(jnp.int32)
        count = count * near
    pl.semaphore_wait(barrier, count - 1)
    send(v_moves[0], X_FACES)
    send(w_moves[0], X_FACES)
    send(v_moves[0], CORNERS)
    guess_part(1)
    guess_part(2)
    send(v_moves[0], Y_FACES)
    send(w_moves[0], Y_FACES)

    def coarsened(source, k, i):
        rows = shapes[k][1]
        held = ts[k - 1]
        held[i] = source
        pair = held[i, pl.ds(0, rows, stride=2)] + held[i, pl.ds(1, rows, stride=2)]
        return 0.5 * depth_sum(pair, 1 << (k - 1))

    for k in range(1, levels + 1):

        def scales(i, k=k):
            coef = coarsened(cs[k - 1][2 * i] + cs[k - 1][2 * i + 1], k, i)
            cs[k][i] = coef
            ws[k][i + WIDE, pl.ds(TOP, shapes[k][1])] = OMEGA / (6.0 + coef)

        loop(0, shapes[k][0], scales)
        send(w_moves[k], list(w_moves[k]))

    fine_rows = pl.ds(TOP - EDGE, ny + 2 * EDGE)

    def smooth_fine(i):
        own, total = around(vs[0], i, TOP - EDGE, ny + 2 * EDGE, 1)
        ps[i, fine_rows] = 1.2 * own + ws[0][i, fine_rows] * total
        return total[EDGE : EDGE + ny]

    def smooth_own(i):
        total = smooth_fine(i + WIDE)
        bs[0][i] = 0.04 * rhs_ref[i] - OMEGA * total

    def fine_residual(i):
        own, total = around(ps, i + WIDE, TOP, ny, 1)
        at = i + WIDE
        fs[0][at, own_rows] = 0.2 * own + (vs[0][at, own_rows] + ws[0][at, own_rows] * total)
        return bs[0][i] + total

    def cuts(k, first, rows):
        span = 1 << k
        low = (agg % span != 0).astype(jnp.float32)
        high = ((agg + 1) % span != 0).astype(jnp.float32)
        row = first + lax.broadcasted_iota(jnp.int32, (rows, nz), 0)
        end = TOP + shapes[k][1]
        up = jnp.where(row == TOP, low, jnp.where(row == end, high, 1.0))
        down = jnp.where(row == TOP - 1, low, jnp.where(row == end - 1, high, 1.0))
        return up, down

    def relax(k):
        ky = shapes[k][1]
        cut = cuts(k, TOP - EDGE, ky + 2 * EDGE)
        rows = pl.ds(TOP - EDGE, ky + 2 * EDGE)

        def body(i):
            own, total = around(vs[k], i, TOP - EDGE, ky + 2 * EDGE, 1 << k, cut)
            result = 1.2 * own + ws[k][i, rows] * total
            if k == levels:
                spread(k, i, result)
            else:
                fs[k][i, rows] = result

        loop(1, shapes[k][0] + WIDE + 1, body)

    def spread(k, i, error):
        count = shapes[k][1] + 2 * EDGE
        us[k - 1][i, pl.ds(0, count, stride=2)] = error
        us[k - 1][i, pl.ds(1, count, stride=2)] = error

    for k in range(1, levels + 1):
        kx, ky, _ = shapes[k]
        if k == 1:
            residual = fine_residual
        else:
            cut = cuts(k - 1, TOP, shapes[k - 1][1])

            def residual(i, k=k, cut=cut):
                _, total = around(
                    vs[k - 1], i + WIDE, TOP, shapes[k - 1][1], 1 << (k - 1), cut
                )
                return 0.2 * bs[k - 1][i] + total

        def descend(i, k=k, residual=residual):
            source = coarsened(residual(2 * i) + residual(2 * i + 1), k, i)
            bs[k][i] = source
            rows = pl.ds(TOP, shapes[k][1])
            vs[k][i + WIDE, rows] = ws[k][i + WIDE, rows] * source

        receive(v_moves[k - 1], Y_FACES)
        if k == 1:
            receive(w_moves[0], Y_FACES)
            loop(1, nx - 1, smooth_own)
        loop(1, kx - 1, descend)
        receive(v_moves[k - 1], X_FACES)
        if k == 1:
            receive(v_moves[0], CORNERS)
            receive(w_moves[0], X_FACES)
            smooth_fine(WIDE - 1)
            smooth_own(0)
            smooth_own(nx - 1)
            smooth_fine(nx + WIDE)
        descend(0)
        descend(kx - 1)
        send(v_moves[k], X_FACES + Y_FACES + CORNERS)
        if k > 1:
            receive(v_moves[k - 1], CORNERS)
            receive(w_moves[k - 1], list(w_moves[k - 1]))
            relax(k - 1)

    receive(w_moves[levels], list(w_moves[levels]))
    receive(v_moves[levels], SIDES)
    relax(levels)

    for k in range(levels - 1, -1, -1):
        kx, ky, _ = shapes[k]
        over = EDGE if k else 0
        count = ky + 2 * over
        rows = pl.ds(TOP - over, count)
        cut = cuts(k, TOP - over, count) if k else None

        def correct(i, k=k, count=count, rows=rows, cut=cut, over=over):
            coarse = us[k]
            own = coarse[i, rows]
            up = coarse[i, pl.ds(TOP - over - 1, count)]
            down = coarse[i, pl.ds(TOP - over + 1, count)]
            if cut is not None:
                up = up * cut[0]
                down = down * cut[1]
            inner = own + (up + down) + depth_pair(own, 1 << k)
            for j in range(2):
                at = 2 * (i - 1) + j
                total = inner + coarse[i - 1 + 2 * j, rows]
                result = fs[k][at, rows] + (0.2 * own + ws[k][at, rows] * total)
                if k == 0:
                    out_ref[at - WIDE] = result
                else:
                    spread(k, at, result)

        if k == 0:
            stores = []
            for q in range(4):
                loop(WIDE + q * part // 2, WIDE + (q + 1) * part // 2, correct)
                planes = pl.ds(q * part, part)
                stores.append(
                    pltpu.make_async_copy(
                        out_ref.at[planes], out_hbm.at[planes], store_sem.at[q]
                    )
                )
                stores[q].start()
        else:
            loop(1, kx // 2 + WIDE + 1, correct)

    for copy in stores:
        copy.wait()

    for copies in v_moves + w_moves:
        for (dx, dy), copy in copies.items():

            @pl.when(inside(dx, dy))
            def _():
                copy.wait_send()


def shards(right_side, coefficient):
    levels = lax.axis_size("agg").bit_length() - 1
    nx, ny, nz = right_side.shape
    shapes = [(nx >> k, ny >> k, nz) for k in range(levels + 1)]
    vmem = lambda shape: pltpu.VMEM(shape, jnp.float32)
    padded = [vmem(padded_shape(*shape)) for shape in shapes]
    plain = [vmem(shape) for shape in shapes]
    halves = [vmem((shapes[k + 1][0], shapes[k][1], nz)) for k in range(levels)]
    spreads = [
        vmem((shapes[k + 1][0] + 2 * WIDE, shapes[k][1] + 2 * TOP, nz)) for k in range(levels)
    ]
    moves = 16 * (levels + 1)
    sems = [pltpu.SemaphoreType.DMA((moves,))] * 2 + [pltpu.SemaphoreType.DMA((8,)), pltpu.SemaphoreType.DMA((4,))]
    cells = nx * ny * nz
    return pl.pallas_call(
        functools.partial(kernel, levels),
        out_shape=jax.ShapeDtypeStruct(right_side.shape, right_side.dtype),
        in_specs=[pl.BlockSpec(memory_space=pltpu.HBM)] * 2,
        out_specs=pl.BlockSpec(memory_space=pltpu.HBM),
        scratch_shapes=padded * 3 + plain * 2 + halves + spreads + [padded[0], plain[0]] + sems,
        compiler_params=pltpu.CompilerParams(
            collective_id=0, has_side_effects=True, vmem_limit_bytes=60 * 2**20
        ),
        cost_estimate=pl.CostEstimate(
            flops=60 * cells, bytes_accessed=12 * cells, transcendentals=0
        ),
        name="vcycle",
    )(right_side, coefficient)


def solution(mesh):
    placed = (P("blk", "agg", None), P("blk", "agg", None))
    return jax.shard_map(
        shards, mesh=mesh, in_specs=placed, out_specs=P("blk", "agg", None), check_vma=False
    )
```

```python
import functools

import jax
import jax.numpy as jnp
from jax import lax
from jax.experimental import pallas as pl
from jax.experimental.pallas import tpu as pltpu
from jax.sharding import PartitionSpec as P

OMEGA = 0.8
WIDE = 2
EDGE = 8
TOP = 16

SIDES = [(dx, dy) for dx in (-1, 0, 1) for dy in (-1, 0, 1) if (dx, dy) != (0, 0)]


def padded_shape(nx, ny, nz):
    return (nx + 2 * WIDE, ny + 2 * TOP, nz)


def depth_pair(field, step):
    axis = field.ndim - 1
    depth = field.shape[axis]
    column = lax.broadcasted_iota(jnp.int32, field.shape, axis)
    ahead = jnp.where(column < depth - step, pltpu.roll(field, depth - step, axis), 0.0)
    behind = jnp.where(column >= step, pltpu.roll(field, step, axis), 0.0)
    return ahead + behind


def depth_sum(field, step):
    axis = field.ndim - 1
    depth = field.shape[axis]
    column = lax.broadcasted_iota(jnp.int32, field.shape, axis)
    ahead = pltpu.roll(field, depth - step, axis)
    behind = pltpu.roll(field, step, axis)
    return field + jnp.where((column // step) % 2 == 0, ahead, behind)


def around(ref, i, first, count, step, cut=None):
    rows = pl.ds(first, count)
    own = ref[i, rows]
    up = ref[i, pl.ds(first - 1, count)]
    down = ref[i, pl.ds(first + 1, count)]
    if cut is not None:
        up = up * cut[0]
        down = down * cut[1]
    total = ref[i - 1, rows] + ref[i + 1, rows] + (up + down)
    return own, total + depth_pair(own, step)


UNROLL = 4


def loop(low, high, body, unroll=UNROLL):
    trips = high - low
    if trips <= unroll:
        for i in range(low, high):
            body(i)
        return
    while trips % unroll:
        unroll -= 1

    def step(i, carry):
        for j in range(unroll):
            body(low + i * unroll + j)
        return carry

    lax.fori_loop(0, trips // unroll, step, 0)


X_FACES = [(-1, 0), (1, 0)]
Y_FACES = [(0, -1), (0, 1)]
CORNERS = [(-1, -1), (-1, 1), (1, -1), (1, 1)]


def halo_copies(ref, nx, ny, wide, corners, sems, base):
    copies = {}
    blk, agg = lax.axis_index("blk"), lax.axis_index("agg")
    for dx, dy in SIDES:
        planes = wide
        if dx != 0 and dy != 0:
            if not corners:
                continue
            planes = corners
        x_from, x_to, x_count = {
            -1: (WIDE, nx + WIDE, planes),
            0: (WIDE, WIDE, nx),
            1: (nx + WIDE - planes, WIDE - planes, planes),
        }[dx]
        y_from, y_to, y_count = {
            -1: (TOP, TOP + ny, EDGE),
            0: (TOP, TOP, ny),
            1: (TOP + ny - EDGE, TOP - EDGE, EDGE),
        }[dy]
        at = base + len(copies)
        copy = pltpu.make_async_remote_copy(
            src_ref=ref.at[pl.ds(x_from, x_count), pl.ds(y_from, y_count)],
            dst_ref=ref.at[pl.ds(x_to, x_count), pl.ds(y_to, y_count)],
            send_sem=sems[0].at[at],
            recv_sem=sems[1].at[at],
            device_id={"blk": blk + dx, "agg": agg + dy},
            device_id_type=pl.DeviceIdType.MESH,
        )
        copies[dx, dy] = copy
    return copies


def kernel(levels, *refs):
    refs = list(refs)
    rhs_hbm, coef_hbm, out_ref = refs[:3]
    refs = refs[3:]
    take = lambda count: [refs.pop(0) for _ in range(count)]
    vs = take(levels + 1)
    ws = take(levels + 1)
    fs = take(levels + 1)
    bs = take(levels + 1)
    cs = take(levels + 1)
    ts = take(levels)
    us = take(levels)
    ps, rhs_ref = take(2)
    coef_ref = cs[0]
    send_sem, recv_sem, load_sem = take(3)

    nx, ny, nz = rhs_ref.shape
    shapes = [(nx >> k, ny >> k, nz) for k in range(levels + 1)]
    blk, agg = lax.axis_index("blk"), lax.axis_index("agg")
    n_blk, n_agg = lax.axis_size("blk"), lax.axis_size("agg")

    part = nx // 4
    loads = {}
    for at, q in enumerate((0, 3, 1, 2)):
        planes = pl.ds(q * part, part)
        loads[q] = [
            pltpu.make_async_copy(hbm.at[planes], ref.at[planes], load_sem.at[2 * at + j])
            for j, (hbm, ref) in enumerate(((coef_hbm, coef_ref), (rhs_hbm, rhs_ref)))
        ]
        for copy in loads[q]:
            copy.start()

    def inside(dx, dy):
        ok = None
        for d, at, size in ((dx, blk, n_blk), (dy, agg, n_agg)):
            if d == 0:
                continue
            this = at > 0 if d < 0 else at < size - 1
            ok = this if ok is None else jnp.logical_and(ok, this)
        return ok

    barrier = pltpu.get_barrier_semaphore()
    for dx, dy in SIDES:

        @pl.when(inside(dx, dy))
        def _():
            pl.semaphore_signal(
                barrier,
                inc=1,
                device_id={"blk": blk + dx, "agg": agg + dy},
                device_id_type=pl.DeviceIdType.MESH,
            )

    @pl.when(blk == 0)
    def _():
        for ref in vs + ws:
            ref[0:WIDE] = jnp.zeros((WIDE,) + ref.shape[1:], jnp.float32)

    @pl.when(blk == n_blk - 1)
    def _():
        for ref in vs + ws:
            high = ref.shape[0]
            ref[high - WIDE : high] = jnp.zeros((WIDE,) + ref.shape[1:], jnp.float32)

    @pl.when(agg == 0)
    def _():
        for ref in vs + ws:
            zero = jnp.zeros((ref.shape[0], EDGE, nz), jnp.float32)
            ref[:, TOP - EDGE : TOP] = zero

    @pl.when(agg == n_agg - 1)
    def _():
        for ref in vs + ws:
            high = ref.shape[1] - TOP
            zero = jnp.zeros((ref.shape[0], EDGE, nz), jnp.float32)
            ref[:, high : high + EDGE] = zero

    used = 0
    v_moves, w_moves = [], []
    for k in range(levels + 1):
        for ref, moves, planes, corners in (
            (vs[k], v_moves, WIDE, WIDE if k > 1 else 1),
            (ws[k], w_moves, 1, 1 if k > 1 else 0),
        ):
            copies = halo_copies(
                ref, *shapes[k][:2], planes, corners, (send_sem, recv_sem), used
            )
            moves.append(copies)
            used += len(copies)

    def send(copies, sides):
        for dx, dy in sides:

            @pl.when(inside(dx, dy))
            def _():
                copies[dx, dy].start()

    def receive(copies, sides):
        for dx, dy in sides:

            @pl.when(inside(-dx, -dy))
            def _():
                copies[dx, dy].wait_recv()

    own_rows = pl.ds(TOP, ny)

    def guess(i):
        scale = OMEGA / (6.0 + coef_ref[i])
        ws[0][i + WIDE, own_rows] = scale
        vs[0][i + WIDE, own_rows] = scale * rhs_ref[i]

    def guess_part(q):
        for copy in loads[q]:
            copy.wait()
        loop(q * part, (q + 1) * part, guess)

    guess_part(0)
    guess_part(3)
    count = 1
    for size, at in ((n_blk, blk), (n_agg, agg)):
        near = 1 + (at > 0).astype(jnp.int32) + (at < size - 1).astype(jnp.int32)
        count = count * near
    pl.semaphore_wait(barrier, count - 1)
    send(v_moves[0], X_FACES)
    send(w_moves[0], X_FACES)
    send(v_moves[0], CORNERS)
    guess_part(1)
    guess_part(2)
    send(v_moves[0], Y_FACES)
    send(w_moves[0], Y_FACES)

    def coarsened(source, k, i):
        rows = shapes[k][1]
        held = ts[k - 1]
        held[i] = source
        pair = held[i, pl.ds(0, rows, stride=2)] + held[i, pl.ds(1, rows, stride=2)]
        return 0.5 * depth_sum(pair, 1 << (k - 1))

    for k in range(1, levels + 1):

        def scales(i, k=k):
            coef = coarsened(cs[k - 1][2 * i] + cs[k - 1][2 * i + 1], k, i)
            cs[k][i] = coef
            ws[k][i + WIDE, pl.ds(TOP, shapes[k][1])] = OMEGA / (6.0 + coef)

        loop(0, shapes[k][0], scales)
        send(w_moves[k], list(w_moves[k]))

    fine_rows = pl.ds(TOP - EDGE, ny + 2 * EDGE)

    def smooth_fine(i):
        own, total = around(vs[0], i, TOP - EDGE, ny + 2 * EDGE, 1)
        ps[i, fine_rows] = 1.2 * own + ws[0][i, fine_rows] * total
        return total[EDGE : EDGE + ny]

    def smooth_own(i):
        total = smooth_fine(i + WIDE)
        bs[0][i] = 0.04 * rhs_ref[i] - OMEGA * total

    def fine_residual(i):
        own, total = around(ps, i + WIDE, TOP, ny, 1)
        at = i + WIDE
        fs[0][at, own_rows] = 0.2 * own + (vs[0][at, own_rows] + ws[0][at, own_rows] * total)
        return bs[0][i] + total

    def cuts(k, first, rows):
        span = 1 << k
        low = (agg % span != 0).astype(jnp.float32)
        high = ((agg + 1) % span != 0).astype(jnp.float32)
        row = first + lax.broadcasted_iota(jnp.int32, (rows, nz), 0)
        end = TOP + shapes[k][1]
        up = jnp.where(row == TOP, low, jnp.where(row == end, high, 1.0))
        down = jnp.where(row == TOP - 1, low, jnp.where(row == end - 1, high, 1.0))
        return up, down

    def relax(k):
        ky = shapes[k][1]
        cut = cuts(k, TOP - EDGE, ky + 2 * EDGE)
        rows = pl.ds(TOP - EDGE, ky + 2 * EDGE)

        def body(i):
            own, total = around(vs[k], i, TOP - EDGE, ky + 2 * EDGE, 1 << k, cut)
            result = 1.2 * own + ws[k][i, rows] * total
            if k == levels:
                spread(k, i, result)
            else:
                fs[k][i, rows] = result

        loop(1, shapes[k][0] + WIDE + 1, body)

    def spread(k, i, error):
        count = shapes[k][1] + 2 * EDGE
        us[k - 1][i, pl.ds(0, count, stride=2)] = error
        us[k - 1][i, pl.ds(1, count, stride=2)] = error

    for k in range(1, levels + 1):
        kx, ky, _ = shapes[k]
        if k == 1:
            residual = fine_residual
        else:
            cut = cuts(k - 1, TOP, shapes[k - 1][1])

            def residual(i, k=k, cut=cut):
                _, total = around(
                    vs[k - 1], i + WIDE, TOP, shapes[k - 1][1], 1 << (k - 1), cut
                )
                return 0.2 * bs[k - 1][i] + total

        def descend(i, k=k, residual=residual):
            source = coarsened(residual(2 * i) + residual(2 * i + 1), k, i)
            bs[k][i] = source
            rows = pl.ds(TOP, shapes[k][1])
            vs[k][i + WIDE, rows] = ws[k][i + WIDE, rows] * source

        receive(v_moves[k - 1], Y_FACES)
        if k == 1:
            receive(w_moves[0], Y_FACES)
            loop(1, nx - 1, smooth_own)
        loop(1, kx - 1, descend)
        receive(v_moves[k - 1], X_FACES)
        if k == 1:
            receive(v_moves[0], CORNERS)
            receive(w_moves[0], X_FACES)
            smooth_fine(WIDE - 1)
            smooth_own(0)
            smooth_own(nx - 1)
            smooth_fine(nx + WIDE)
        descend(0)
        descend(kx - 1)
        send(v_moves[k], X_FACES + Y_FACES + CORNERS)
        if k > 1:
            receive(v_moves[k - 1], CORNERS)
            receive(w_moves[k - 1], list(w_moves[k - 1]))
            relax(k - 1)

    receive(w_moves[levels], list(w_moves[levels]))
    receive(v_moves[levels], SIDES)
    relax(levels)

    for k in range(levels - 1, -1, -1):
        kx, ky, _ = shapes[k]
        over = EDGE if k else 0
        count = ky + 2 * over
        rows = pl.ds(TOP - over, count)
        cut = cuts(k, TOP - over, count) if k else None

        def correct(i, k=k, count=count, rows=rows, cut=cut, over=over):
            coarse = us[k]
            own = coarse[i, rows]
            up = coarse[i, pl.ds(TOP - over - 1, count)]
            down = coarse[i, pl.ds(TOP - over + 1, count)]
            if cut is not None:
                up = up * cut[0]
                down = down * cut[1]
            inner = own + (up + down) + depth_pair(own, 1 << k)
            for j in range(2):
                at = 2 * (i - 1) + j
                total = inner + coarse[i - 1 + 2 * j, rows]
                result = fs[k][at, rows] + (0.2 * own + ws[k][at, rows] * total)
                if k == 0:
                    out_ref[at - WIDE] = result
                else:
                    spread(k, at, result)

        if k == 0:
            loop(WIDE, kx // 2 + WIDE, correct)
        else:
            loop(1, kx // 2 + WIDE + 1, correct)

    for copies in v_moves + w_moves:
        for (dx, dy), copy in copies.items():

            @pl.when(inside(dx, dy))
            def _():
                copy.wait_send()


def shards(right_side, coefficient):
    levels = lax.axis_size("agg").bit_length() - 1
    nx, ny, nz = right_side.shape
    shapes = [(nx >> k, ny >> k, nz) for k in range(levels + 1)]
    vmem = lambda shape: pltpu.VMEM(shape, jnp.float32)
    padded = [vmem(padded_shape(*shape)) for shape in shapes]
    plain = [vmem(shape) for shape in shapes]
    halves = [vmem((shapes[k + 1][0], shapes[k][1], nz)) for k in range(levels)]
    spreads = [
        vmem((shapes[k + 1][0] + 2 * WIDE, shapes[k][1] + 2 * TOP, nz)) for k in range(levels)
    ]
    moves = 16 * (levels + 1)
    sems = [pltpu.SemaphoreType.DMA((moves,))] * 2 + [pltpu.SemaphoreType.DMA((8,))]
    cells = nx * ny * nz
    return pl.pallas_call(
        functools.partial(kernel, levels),
        out_shape=pltpu.VMEM(right_side.shape, right_side.dtype),
        in_specs=[pl.BlockSpec(memory_space=pltpu.HBM)] * 2,
        out_specs=pl.BlockSpec(memory_space=pltpu.VMEM),
        scratch_shapes=padded * 3 + plain * 2 + halves + spreads + [padded[0], plain[0]] + sems,
        compiler_params=pltpu.CompilerParams(
            collective_id=0, has_side_effects=True, vmem_limit_bytes=58 * 2**20
        ),
        cost_estimate=pl.CostEstimate(
            flops=60 * cells, bytes_accessed=12 * cells, transcendentals=0
        ),
        name="vcycle",
    )(right_side, coefficient)


def solution(mesh):
    placed = (P("blk", "agg", None), P("blk", "agg", None))
    return jax.shard_map(
        shards, mesh=mesh, in_specs=placed, out_specs=P("blk", "agg", None), check_vma=False
    )
```

```python
import functools

import jax
import jax.numpy as jnp
from jax import lax
from jax.experimental import pallas as pl
from jax.experimental.pallas import tpu as pltpu
from jax.sharding import PartitionSpec as P

OMEGA = 0.8
WIDE = 2
EDGE = 8
TOP = 16

SIDES = [(dx, dy) for dx in (-1, 0, 1) for dy in (-1, 0, 1) if (dx, dy) != (0, 0)]


def padded_shape(nx, ny, nz):
    return (nx + 2 * WIDE, ny + 2 * TOP, nz)


def depth_pair(field, step):
    axis = field.ndim - 1
    depth = field.shape[axis]
    column = lax.broadcasted_iota(jnp.int32, field.shape, axis)
    ahead = jnp.where(column < depth - step, pltpu.roll(field, depth - step, axis), 0.0)
    behind = jnp.where(column >= step, pltpu.roll(field, step, axis), 0.0)
    return ahead + behind


def depth_sum(field, step):
    axis = field.ndim - 1
    depth = field.shape[axis]
    column = lax.broadcasted_iota(jnp.int32, field.shape, axis)
    ahead = pltpu.roll(field, depth - step, axis)
    behind = pltpu.roll(field, step, axis)
    return field + jnp.where((column // step) % 2 == 0, ahead, behind)


def around(ref, i, first, count, step, cut=None):
    rows = pl.ds(first, count)
    own = ref[i, rows]
    up = ref[i, pl.ds(first - 1, count)]
    down = ref[i, pl.ds(first + 1, count)]
    if cut is not None:
        up = up * cut[0]
        down = down * cut[1]
    total = ref[i - 1, rows] + ref[i + 1, rows] + (up + down)
    return own, total + depth_pair(own, step)


UNROLL = 8


def loop(low, high, body, unroll=UNROLL):
    trips = high - low
    if trips <= unroll:
        for i in range(low, high):
            body(i)
        return
    while trips % unroll:
        unroll -= 1

    def step(i, carry):
        for j in range(unroll):
            body(low + i * unroll + j)
        return carry

    lax.fori_loop(0, trips // unroll, step, 0)


X_FACES = [(-1, 0), (1, 0)]
Y_FACES = [(0, -1), (0, 1)]
CORNERS = [(-1, -1), (-1, 1), (1, -1), (1, 1)]


def halo_copies(ref, nx, ny, wide, corners, sems, base):
    copies = {}
    blk, agg = lax.axis_index("blk"), lax.axis_index("agg")
    for dx, dy in SIDES:
        planes = wide
        if dx != 0 and dy != 0:
            if not corners:
                continue
            planes = corners
        x_from, x_to, x_count = {
            -1: (WIDE, nx + WIDE, planes),
            0: (WIDE, WIDE, nx),
            1: (nx + WIDE - planes, WIDE - planes, planes),
        }[dx]
        y_from, y_to, y_count = {
            -1: (TOP, TOP + ny, EDGE),
            0: (TOP, TOP, ny),
            1: (TOP + ny - EDGE, TOP - EDGE, EDGE),
        }[dy]
        at = base + len(copies)
        copy = pltpu.make_async_remote_copy(
            src_ref=ref.at[pl.ds(x_from, x_count), pl.ds(y_from, y_count)],
            dst_ref=ref.at[pl.ds(x_to, x_count), pl.ds(y_to, y_count)],
            send_sem=sems[0].at[at],
            recv_sem=sems[1].at[at],
            device_id={"blk": blk + dx, "agg": agg + dy},
            device_id_type=pl.DeviceIdType.MESH,
        )
        copies[dx, dy] = copy
    return copies


def kernel(levels, *refs):
    refs = list(refs)
    rhs_hbm, coef_hbm, out_ref = refs[:3]
    refs = refs[3:]
    take = lambda count: [refs.pop(0) for _ in range(count)]
    vs = take(levels + 1)
    ws = take(levels + 1)
    fs = take(levels + 1)
    bs = take(levels + 1)
    cs = take(levels + 1)
    ts = take(levels)
    us = take(levels)
    ps, rhs_ref = take(2)
    coef_ref = cs[0]
    send_sem, recv_sem, load_sem = take(3)

    nx, ny, nz = rhs_ref.shape
    shapes = [(nx >> k, ny >> k, nz) for k in range(levels + 1)]
    blk, agg = lax.axis_index("blk"), lax.axis_index("agg")
    n_blk, n_agg = lax.axis_size("blk"), lax.axis_size("agg")

    part = nx // 4
    loads = {}
    for at, q in enumerate((0, 3, 1, 2)):
        planes = pl.ds(q * part, part)
        loads[q] = [
            pltpu.make_async_copy(hbm.at[planes], ref.at[planes], load_sem.at[2 * at + j])
            for j, (hbm, ref) in enumerate(((coef_hbm, coef_ref), (rhs_hbm, rhs_ref)))
        ]
        for copy in loads[q]:
            copy.start()

    def inside(dx, dy):
        ok = None
        for d, at, size in ((dx, blk, n_blk), (dy, agg, n_agg)):
            if d == 0:
                continue
            this = at > 0 if d < 0 else at < size - 1
            ok = this if ok is None else jnp.logical_and(ok, this)
        return ok

    barrier = pltpu.get_barrier_semaphore()
    for dx, dy in SIDES:

        @pl.when(inside(dx, dy))
        def _():
            pl.semaphore_signal(
                barrier,
                inc=1,
                device_id={"blk": blk + dx, "agg": agg + dy},
                device_id_type=pl.DeviceIdType.MESH,
            )

    @pl.when(blk == 0)
    def _():
        for ref in vs + ws:
            ref[0:WIDE] = jnp.zeros((WIDE,) + ref.shape[1:], jnp.float32)

    @pl.when(blk == n_blk - 1)
    def _():
        for ref in vs + ws:
            high = ref.shape[0]
            ref[high - WIDE : high] = jnp.zeros((WIDE,) + ref.shape[1:], jnp.float32)

    @pl.when(agg == 0)
    def _():
        for ref in vs + ws:
            zero = jnp.zeros((ref.shape[0], EDGE, nz), jnp.float32)
            ref[:, TOP - EDGE : TOP] = zero

    @pl.when(agg == n_agg - 1)
    def _():
        for ref in vs + ws:
            high = ref.shape[1] - TOP
            zero = jnp.zeros((ref.shape[0], EDGE, nz), jnp.float32)
            ref[:, high : high + EDGE] = zero

    used = 0
    v_moves, w_moves = [], []
    for k in range(levels + 1):
        for ref, moves, planes, corners in (
            (vs[k], v_moves, WIDE, WIDE if k > 1 else 1),
            (ws[k], w_moves, 1, 1 if k > 1 else 0),
        ):
            copies = halo_copies(
                ref, *shapes[k][:2], planes, corners, (send_sem, recv_sem), used
            )
            moves.append(copies)
            used += len(copies)

    def send(copies, sides):
        for dx, dy in sides:

            @pl.when(inside(dx, dy))
            def _():
                copies[dx, dy].start()

    def receive(copies, sides):
        for dx, dy in sides:

            @pl.when(inside(-dx, -dy))
            def _():
                copies[dx, dy].wait_recv()

    own_rows = pl.ds(TOP, ny)

    def guess(i):
        scale = OMEGA / (6.0 + coef_ref[i])
        ws[0][i + WIDE, own_rows] = scale
        vs[0][i + WIDE, own_rows] = scale * rhs_ref[i]

    def guess_part(q):
        for copy in loads[q]:
            copy.wait()
        loop(q * part, (q + 1) * part, guess)

    guess_part(0)
    guess_part(3)
    count = 1
    for size, at in ((n_blk, blk), (n_agg, agg)):
        near = 1 + (at > 0).astype(jnp.int32) + (at < size - 1).astype(jnp.int32)
        count = count * near
    pl.semaphore_wait(barrier, count - 1)
    send(v_moves[0], X_FACES)
    send(w_moves[0], X_FACES)
    send(v_moves[0], CORNERS)
    guess_part(1)
    guess_part(2)
    send(v_moves[0], Y_FACES)
    send(w_moves[0], Y_FACES)

    def coarsened(source, k, i):
        rows = shapes[k][1]
        held = ts[k - 1]
        held[i] = source
        pair = held[i, pl.ds(0, rows, stride=2)] + held[i, pl.ds(1, rows, stride=2)]
        return 0.5 * depth_sum(pair, 1 << (k - 1))

    for k in range(1, levels + 1):

        def scales(i, k=k):
            coef = coarsened(cs[k - 1][2 * i] + cs[k - 1][2 * i + 1], k, i)
            cs[k][i] = coef
            ws[k][i + WIDE, pl.ds(TOP, shapes[k][1])] = OMEGA / (6.0 + coef)

        loop(0, shapes[k][0], scales)
        send(w_moves[k], list(w_moves[k]))

    fine_rows = pl.ds(TOP - EDGE, ny + 2 * EDGE)

    def smooth_fine(i):
        own, total = around(vs[0], i, TOP - EDGE, ny + 2 * EDGE, 1)
        ps[i, fine_rows] = 1.2 * own + ws[0][i, fine_rows] * total
        return total[EDGE : EDGE + ny]

    def smooth_own(i):
        total = smooth_fine(i + WIDE)
        bs[0][i] = 0.04 * rhs_ref[i] - OMEGA * total

    def fine_residual(i):
        own, total = around(ps, i + WIDE, TOP, ny, 1)
        at = i + WIDE
        fs[0][at, own_rows] = 0.2 * own + (vs[0][at, own_rows] + ws[0][at, own_rows] * total)
        return bs[0][i] + total

    def cuts(k, first, rows):
        span = 1 << k
        low = (agg % span != 0).astype(jnp.float32)
        high = ((agg + 1) % span != 0).astype(jnp.float32)
        row = first + lax.broadcasted_iota(jnp.int32, (rows, nz), 0)
        end = TOP + shapes[k][1]
        up = jnp.where(row == TOP, low, jnp.where(row == end, high, 1.0))
        down = jnp.where(row == TOP - 1, low, jnp.where(row == end - 1, high, 1.0))
        return up, down

    def relax(k):
        ky = shapes[k][1]
        cut = cuts(k, TOP - EDGE, ky + 2 * EDGE)
        rows = pl.ds(TOP - EDGE, ky + 2 * EDGE)

        def body(i):
            own, total = around(vs[k], i, TOP - EDGE, ky + 2 * EDGE, 1 << k, cut)
            result = 1.2 * own + ws[k][i, rows] * total
            if k == levels:
                spread(k, i, result)
            else:
                fs[k][i, rows] = result

        loop(1, shapes[k][0] + WIDE + 1, body)

    def spread(k, i, error):
        count = shapes[k][1] + 2 * EDGE
        us[k - 1][i, pl.ds(0, count, stride=2)] = error
        us[k - 1][i, pl.ds(1, count, stride=2)] = error

    for k in range(1, levels + 1):
        kx, ky, _ = shapes[k]
        if k == 1:
            residual = fine_residual
        else:
            cut = cuts(k - 1, TOP, shapes[k - 1][1])

            def residual(i, k=k, cut=cut):
                _, total = around(
                    vs[k - 1], i + WIDE, TOP, shapes[k - 1][1], 1 << (k - 1), cut
                )
                return 0.2 * bs[k - 1][i] + total

        def descend(i, k=k, residual=residual):
            source = coarsened(residual(2 * i) + residual(2 * i + 1), k, i)
            bs[k][i] = source
            rows = pl.ds(TOP, shapes[k][1])
            vs[k][i + WIDE, rows] = ws[k][i + WIDE, rows] * source

        receive(v_moves[k - 1], Y_FACES)
        if k == 1:
            receive(w_moves[0], Y_FACES)
            loop(1, nx - 1, smooth_own)
        loop(1, kx - 1, descend)
        receive(v_moves[k - 1], X_FACES)
        if k == 1:
            receive(v_moves[0], CORNERS)
            receive(w_moves[0], X_FACES)
            smooth_fine(WIDE - 1)
            smooth_own(0)
            smooth_own(nx - 1)
            smooth_fine(nx + WIDE)
        descend(0)
        descend(kx - 1)
        send(v_moves[k], X_FACES + Y_FACES + CORNERS)
        if k > 1:
            receive(v_moves[k - 1], CORNERS)
            receive(w_moves[k - 1], list(w_moves[k - 1]))
            relax(k - 1)

    receive(w_moves[levels], list(w_moves[levels]))
    receive(v_moves[levels], SIDES)
    relax(levels)

    for k in range(levels - 1, -1, -1):
        kx, ky, _ = shapes[k]
        over = EDGE if k else 0
        count = ky + 2 * over
        rows = pl.ds(TOP - over, count)
        cut = cuts(k, TOP - over, count) if k else None

        def correct(i, k=k, count=count, rows=rows, cut=cut, over=over):
            coarse = us[k]
            own = coarse[i, rows]
            up = coarse[i, pl.ds(TOP - over - 1, count)]
            down = coarse[i, pl.ds(TOP - over + 1, count)]
            if cut is not None:
                up = up * cut[0]
                down = down * cut[1]
            inner = own + (up + down) + depth_pair(own, 1 << k)
            for j in range(2):
                at = 2 * (i - 1) + j
                total = inner + coarse[i - 1 + 2 * j, rows]
                result = fs[k][at, rows] + (0.2 * own + ws[k][at, rows] * total)
                if k == 0:
                    out_ref[at - WIDE] = result
                else:
                    spread(k, at, result)

        if k == 0:
            loop(WIDE, kx // 2 + WIDE, correct)
        else:
            loop(1, kx // 2 + WIDE + 1, correct)

    for copies in v_moves + w_moves:
        for (dx, dy), copy in copies.items():

            @pl.when(inside(dx, dy))
            def _():
                copy.wait_send()


def shards(right_side, coefficient):
    levels = lax.axis_size("agg").bit_length() - 1
    nx, ny, nz = right_side.shape
    shapes = [(nx >> k, ny >> k, nz) for k in range(levels + 1)]
    vmem = lambda shape: pltpu.VMEM(shape, jnp.float32)
    padded = [vmem(padded_shape(*shape)) for shape in shapes]
    plain = [vmem(shape) for shape in shapes]
    halves = [vmem((shapes[k + 1][0], shapes[k][1], nz)) for k in range(levels)]
    spreads = [
        vmem((shapes[k + 1][0] + 2 * WIDE, shapes[k][1] + 2 * TOP, nz)) for k in range(levels)
    ]
    moves = 16 * (levels + 1)
    sems = [pltpu.SemaphoreType.DMA((moves,))] * 2 + [pltpu.SemaphoreType.DMA((8,))]
    cells = nx * ny * nz
    return pl.pallas_call(
        functools.partial(kernel, levels),
        out_shape=pltpu.VMEM(right_side.shape, right_side.dtype),
        in_specs=[pl.BlockSpec(memory_space=pltpu.HBM)] * 2,
        out_specs=pl.BlockSpec(memory_space=pltpu.VMEM),
        scratch_shapes=padded * 3 + plain * 2 + halves + spreads + [padded[0], plain[0]] + sems,
        compiler_params=pltpu.CompilerParams(
            collective_id=0, has_side_effects=True, vmem_limit_bytes=58 * 2**20
        ),
        cost_estimate=pl.CostEstimate(
            flops=60 * cells, bytes_accessed=12 * cells, transcendentals=0
        ),
        name="vcycle",
    )(right_side, coefficient)


def solution(mesh):
    placed = (P("blk", "agg", None), P("blk", "agg", None))
    return jax.shard_map(
        shards, mesh=mesh, in_specs=placed, out_specs=P("blk", "agg", None), check_vma=False
    )
```

```python
import functools

import jax
import jax.numpy as jnp
from jax import lax
from jax.experimental import pallas as pl
from jax.experimental.pallas import tpu as pltpu
from jax.sharding import PartitionSpec as P

OMEGA = 0.8
WIDE = 2
EDGE = 8
TOP = 16

SIDES = [(dx, dy) for dx in (-1, 0, 1) for dy in (-1, 0, 1) if (dx, dy) != (0, 0)]


def padded_shape(nx, ny, nz):
    return (nx + 2 * WIDE, ny + 2 * TOP, nz)


def depth_pair(field, step):
    axis = field.ndim - 1
    depth = field.shape[axis]
    column = lax.broadcasted_iota(jnp.int32, field.shape, axis)
    ahead = jnp.where(column < depth - step, pltpu.roll(field, depth - step, axis), 0.0)
    behind = jnp.where(column >= step, pltpu.roll(field, step, axis), 0.0)
    return ahead + behind


def depth_sum(field, step):
    axis = field.ndim - 1
    depth = field.shape[axis]
    column = lax.broadcasted_iota(jnp.int32, field.shape, axis)
    ahead = pltpu.roll(field, depth - step, axis)
    behind = pltpu.roll(field, step, axis)
    return field + jnp.where((column // step) % 2 == 0, ahead, behind)


def around(ref, i, first, count, step, cut=None):
    rows = pl.ds(first, count)
    own = ref[i, rows]
    up = ref[i, pl.ds(first - 1, count)]
    down = ref[i, pl.ds(first + 1, count)]
    if cut is not None:
        up = up * cut[0]
        down = down * cut[1]
    total = ref[i - 1, rows] + ref[i + 1, rows] + (up + down)
    return own, total + depth_pair(own, step)


UNROLL = 8


def loop(low, high, body, unroll=UNROLL):
    trips = high - low
    if trips <= unroll:
        for i in range(low, high):
            body(i)
        return
    while trips % unroll:
        unroll -= 1

    def step(i, carry):
        for j in range(unroll):
            body(low + i * unroll + j)
        return carry

    lax.fori_loop(0, trips // unroll, step, 0)


X_FACES = [(-1, 0), (1, 0)]
Y_FACES = [(0, -1), (0, 1)]
CORNERS = [(-1, -1), (-1, 1), (1, -1), (1, 1)]


def halo_copies(ref, nx, ny, wide, corners, sems, base, packed):
    copies = {}
    blk, agg = lax.axis_index("blk"), lax.axis_index("agg")
    for dx, dy in SIDES:
        planes = wide
        if dx != 0 and dy != 0:
            if not corners:
                continue
            planes = corners
        x_from, x_to, x_count = {
            -1: (WIDE, nx + WIDE, planes),
            0: (WIDE, WIDE, nx),
            1: (nx + WIDE - planes, WIDE - planes, planes),
        }[dx]
        y_from, y_to, y_count = {
            -1: (TOP, TOP + ny, EDGE),
            0: (TOP, TOP, ny),
            1: (TOP + ny - EDGE, TOP - EDGE, EDGE),
        }[dy]
        at = base + len(copies)
        source = ref.at[pl.ds(x_from, x_count), pl.ds(y_from, y_count)]
        target = ref.at[pl.ds(x_to, x_count), pl.ds(y_to, y_count)]
        if packed is not None and dy == 0:
            source, target = (packed.at[0], packed.at[3]) if dx < 0 else (packed.at[1], packed.at[2])
        copy = pltpu.make_async_remote_copy(
            src_ref=source,
            dst_ref=target,
            send_sem=sems[0].at[at],
            recv_sem=sems[1].at[at],
            device_id={"blk": blk + dx, "agg": agg + dy},
            device_id_type=pl.DeviceIdType.MESH,
        )
        copies[dx, dy] = copy
    return copies


def kernel(levels, *refs):
    refs = list(refs)
    rhs_hbm, coef_hbm, out_ref = refs[:3]
    refs = refs[3:]
    take = lambda count: [refs.pop(0) for _ in range(count)]
    vs = take(levels + 1)
    ws = take(levels + 1)
    fs = take(levels + 1)
    bs = take(levels + 1)
    cs = take(levels + 1)
    ts = take(levels)
    us = take(levels)
    ps, rhs_ref = take(2)
    faces = [None] + take(levels)
    coef_ref = cs[0]
    send_sem, recv_sem, load_sem = take(3)

    nx, ny, nz = rhs_ref.shape
    shapes = [(nx >> k, ny >> k, nz) for k in range(levels + 1)]
    blk, agg = lax.axis_index("blk"), lax.axis_index("agg")
    n_blk, n_agg = lax.axis_size("blk"), lax.axis_size("agg")

    part = nx // 4
    loads = {}
    for at, q in enumerate((0, 3, 1, 2)):
        planes = pl.ds(q * part, part)
        loads[q] = [
            pltpu.make_async_copy(hbm.at[planes], ref.at[planes], load_sem.at[2 * at + j])
            for j, (hbm, ref) in enumerate(((coef_hbm, coef_ref), (rhs_hbm, rhs_ref)))
        ]
        for copy in loads[q]:
            copy.start()

    def inside(dx, dy):
        ok = None
        for d, at, size in ((dx, blk, n_blk), (dy, agg, n_agg)):
            if d == 0:
                continue
            this = at > 0 if d < 0 else at < size - 1
            ok = this if ok is None else jnp.logical_and(ok, this)
        return ok

    barrier = pltpu.get_barrier_semaphore()
    for dx, dy in SIDES:

        @pl.when(inside(dx, dy))
        def _():
            pl.semaphore_signal(
                barrier,
                inc=1,
                device_id={"blk": blk + dx, "agg": agg + dy},
                device_id_type=pl.DeviceIdType.MESH,
            )

    @pl.when(blk == 0)
    def _():
        for ref in vs + ws:
            ref[0:WIDE] = jnp.zeros((WIDE,) + ref.shape[1:], jnp.float32)

    @pl.when(blk == n_blk - 1)
    def _():
        for ref in vs + ws:
            high = ref.shape[0]
            ref[high - WIDE : high] = jnp.zeros((WIDE,) + ref.shape[1:], jnp.float32)

    @pl.when(agg == 0)
    def _():
        for ref in vs + ws:
            zero = jnp.zeros((ref.shape[0], EDGE, nz), jnp.float32)
            ref[:, TOP - EDGE : TOP] = zero

    @pl.when(agg == n_agg - 1)
    def _():
        for ref in vs + ws:
            high = ref.shape[1] - TOP
            zero = jnp.zeros((ref.shape[0], EDGE, nz), jnp.float32)
            ref[:, high : high + EDGE] = zero

    used = 0
    v_moves, w_moves = [], []
    for k in range(levels + 1):
        for ref, moves, planes, corners, packed in (
            (vs[k], v_moves, WIDE, WIDE if k > 1 else 1, faces[k]),
            (ws[k], w_moves, 1, 1 if k > 1 else 0, None),
        ):
            copies = halo_copies(
                ref, *shapes[k][:2], planes, corners, (send_sem, recv_sem), used, packed
            )
            moves.append(copies)
            used += len(copies)

    def send(copies, sides):
        for dx, dy in sides:

            @pl.when(inside(dx, dy))
            def _():
                copies[dx, dy].start()

    def receive(copies, sides):
        for dx, dy in sides:

            @pl.when(inside(-dx, -dy))
            def _():
                copies[dx, dy].wait_recv()

    def first_half(k):
        column = lax.broadcasted_iota(jnp.int32, (shapes[k][1], nz), 1)
        return (column >> (k - 1)) % 2 == 0

    def pack_faces(k):
        rows = pl.ds(TOP, shapes[k][1])
        for slot, plane in ((0, WIDE), (1, shapes[k][0])):
            faces[k][slot] = jnp.where(first_half(k), vs[k][plane, rows], vs[k][plane + 1, rows])

    def receive_faces(k):
        rows, half = pl.ds(TOP, shapes[k][1]), 1 << (k - 1)
        for dx, slot, plane in ((1, 2, 0), (-1, 3, shapes[k][0] + WIDE)):

            @pl.when(inside(-dx, 0))
            def _():
                v_moves[k][dx, 0].wait_recv()
                both = faces[k][slot]
                low = first_half(k)
                vs[k][plane, rows] = jnp.where(low, both, pltpu.roll(both, half, 1))
                vs[k][plane + 1, rows] = jnp.where(low, pltpu.roll(both, nz - half, 1), both)

    own_rows = pl.ds(TOP, ny)

    def guess(i):
        scale = OMEGA / (6.0 + coef_ref[i])
        ws[0][i + WIDE, own_rows] = scale
        vs[0][i + WIDE, own_rows] = scale * rhs_ref[i]

    def guess_part(q):
        for copy in loads[q]:
            copy.wait()
        loop(q * part, (q + 1) * part, guess)

    guess_part(0)
    guess_part(3)
    count = 1
    for size, at in ((n_blk, blk), (n_agg, agg)):
        near = 1 + (at > 0).astype(jnp.int32) + (at < size - 1).astype(jnp.int32)
        count = count * near
    pl.semaphore_wait(barrier, count - 1)
    send(v_moves[0], X_FACES)
    send(w_moves[0], X_FACES)
    send(v_moves[0], CORNERS)
    guess_part(1)
    guess_part(2)
    send(v_moves[0], Y_FACES)
    send(w_moves[0], Y_FACES)

    def coarsened(source, k, i):
        rows = shapes[k][1]
        held = ts[k - 1]
        held[i] = source
        pair = held[i, pl.ds(0, rows, stride=2)] + held[i, pl.ds(1, rows, stride=2)]
        return 0.5 * depth_sum(pair, 1 << (k - 1))

    for k in range(1, levels + 1):

        def scales(i, k=k):
            coef = coarsened(cs[k - 1][2 * i] + cs[k - 1][2 * i + 1], k, i)
            cs[k][i] = coef
            ws[k][i + WIDE, pl.ds(TOP, shapes[k][1])] = OMEGA / (6.0 + coef)

        loop(0, shapes[k][0], scales)

    fine_rows = pl.ds(TOP - EDGE, ny + 2 * EDGE)

    def smooth_fine(i):
        own, total = around(vs[0], i, TOP - EDGE, ny + 2 * EDGE, 1)
        ps[i, fine_rows] = 1.2 * own + ws[0][i, fine_rows] * total
        return total[EDGE : EDGE + ny]

    def smooth_own(i):
        total = smooth_fine(i + WIDE)
        bs[0][i] = 0.04 * rhs_ref[i] - OMEGA * total

    def fine_residual(i):
        own, total = around(ps, i + WIDE, TOP, ny, 1)
        at = i + WIDE
        fs[0][at, own_rows] = 0.2 * own + (vs[0][at, own_rows] + ws[0][at, own_rows] * total)
        return bs[0][i] + total

    def cuts(k, first, rows):
        span = 1 << k
        low = (agg % span != 0).astype(jnp.float32)
        high = ((agg + 1) % span != 0).astype(jnp.float32)
        row = first + lax.broadcasted_iota(jnp.int32, (rows, nz), 0)
        end = TOP + shapes[k][1]
        up = jnp.where(row == TOP, low, jnp.where(row == end, high, 1.0))
        down = jnp.where(row == TOP - 1, low, jnp.where(row == end - 1, high, 1.0))
        return up, down

    def relax(k):
        ky = shapes[k][1]
        cut = cuts(k, TOP - EDGE, ky + 2 * EDGE)
        rows = pl.ds(TOP - EDGE, ky + 2 * EDGE)

        def body(i):
            own, total = around(vs[k], i, TOP - EDGE, ky + 2 * EDGE, 1 << k, cut)
            result = 1.2 * own + ws[k][i, rows] * total
            if k == levels:
                spread(k, i, result)
            else:
                fs[k][i, rows] = result

        loop(1, shapes[k][0] + WIDE + 1, body)

    def spread(k, i, error):
        count = shapes[k][1] + 2 * EDGE
        us[k - 1][i, pl.ds(0, count, stride=2)] = error
        us[k - 1][i, pl.ds(1, count, stride=2)] = error

    for k in range(1, levels + 1):
        kx, ky, _ = shapes[k]
        if k == 1:
            residual = fine_residual
        else:
            cut = cuts(k - 1, TOP, shapes[k - 1][1])

            def residual(i, k=k, cut=cut):
                _, total = around(
                    vs[k - 1], i + WIDE, TOP, shapes[k - 1][1], 1 << (k - 1), cut
                )
                return 0.2 * bs[k - 1][i] + total

        def descend(i, k=k, residual=residual):
            source = coarsened(residual(2 * i) + residual(2 * i + 1), k, i)
            bs[k][i] = source
            rows = pl.ds(TOP, shapes[k][1])
            vs[k][i + WIDE, rows] = ws[k][i + WIDE, rows] * source

        receive(v_moves[k - 1], Y_FACES)
        if k == 1:
            receive(w_moves[0], Y_FACES)
            loop(1, nx - 1, smooth_own)
        loop(1, kx - 1, descend)
        if k > 1:
            receive_faces(k - 1)
        else:
            for moves in w_moves[1:]:
                send(moves, list(moves))
            receive(v_moves[0], X_FACES + CORNERS)
            receive(w_moves[0], X_FACES)
            smooth_fine(WIDE - 1)
            smooth_own(0)
            smooth_own(nx - 1)
            smooth_fine(nx + WIDE)
        descend(0)
        descend(kx - 1)
        pack_faces(k)
        send(v_moves[k], X_FACES + Y_FACES + CORNERS)
        if k > 1:
            receive(v_moves[k - 1], CORNERS)
            receive(w_moves[k - 1], list(w_moves[k - 1]))
            relax(k - 1)

    receive(w_moves[levels], list(w_moves[levels]))
    receive(v_moves[levels], Y_FACES + CORNERS)
    receive_faces(levels)
    relax(levels)

    for k in range(levels - 1, -1, -1):
        kx, ky, _ = shapes[k]
        over = EDGE if k else 0
        count = ky + 2 * over
        rows = pl.ds(TOP - over, count)
        cut = cuts(k, TOP - over, count) if k else None

        def correct(i, k=k, count=count, rows=rows, cut=cut, over=over):
            coarse = us[k]
            own = coarse[i, rows]
            up = coarse[i, pl.ds(TOP - over - 1, count)]
            down = coarse[i, pl.ds(TOP - over + 1, count)]
            if cut is not None:
                up = up * cut[0]
                down = down * cut[1]
            inner = own + (up + down) + depth_pair(own, 1 << k)
            for j in range(2):
                at = 2 * (i - 1) + j
                total = inner + coarse[i - 1 + 2 * j, rows]
                result = fs[k][at, rows] + (0.2 * own + ws[k][at, rows] * total)
                if k == 0:
                    out_ref[at - WIDE] = result
                else:
                    spread(k, at, result)

        if k == 0:
            loop(WIDE, kx // 2 + WIDE, correct)
        else:
            loop(1, kx // 2 + WIDE + 1, correct)

    for copies in v_moves + w_moves:
        for (dx, dy), copy in copies.items():

            @pl.when(inside(dx, dy))
            def _():
                copy.wait_send()


def shards(right_side, coefficient):
    levels = lax.axis_size("agg").bit_length() - 1
    nx, ny, nz = right_side.shape
    shapes = [(nx >> k, ny >> k, nz) for k in range(levels + 1)]
    vmem = lambda shape: pltpu.VMEM(shape, jnp.float32)
    padded = [vmem(padded_shape(*shape)) for shape in shapes]
    plain = [vmem(shape) for shape in shapes]
    halves = [vmem((shapes[k + 1][0], shapes[k][1], nz)) for k in range(levels)]
    spreads = [
        vmem((shapes[k + 1][0] + 2 * WIDE, shapes[k][1] + 2 * TOP, nz)) for k in range(levels)
    ]
    faces = [vmem((4,) + shape[1:]) for shape in shapes[1:]]
    moves = 16 * (levels + 1)
    sems = [pltpu.SemaphoreType.DMA((moves,))] * 2 + [pltpu.SemaphoreType.DMA((8,))]
    cells = nx * ny * nz
    return pl.pallas_call(
        functools.partial(kernel, levels),
        out_shape=pltpu.VMEM(right_side.shape, right_side.dtype),
        in_specs=[pl.BlockSpec(memory_space=pltpu.HBM)] * 2,
        out_specs=pl.BlockSpec(memory_space=pltpu.VMEM),
        scratch_shapes=padded * 3 + plain * 2 + halves + spreads + [padded[0], plain[0]] + faces + sems,
        compiler_params=pltpu.CompilerParams(
            collective_id=0, has_side_effects=True, vmem_limit_bytes=58 * 2**20
        ),
        cost_estimate=pl.CostEstimate(
            flops=60 * cells, bytes_accessed=12 * cells, transcendentals=0
        ),
        name="vcycle",
    )(right_side, coefficient)


def solution(mesh):
    placed = (P("blk", "agg", None), P("blk", "agg", None))
    return jax.shard_map(
        shards, mesh=mesh, in_specs=placed, out_specs=P("blk", "agg", None), check_vma=False
    )
```

```python
import functools

import jax
import jax.numpy as jnp
from jax import lax
from jax.experimental import pallas as pl
from jax.experimental.pallas import tpu as pltpu
from jax.sharding import PartitionSpec as P

OMEGA = 0.8
WIDE = 2
EDGE = 8
TOP = 16

SIDES = [(dx, dy) for dx in (-1, 0, 1) for dy in (-1, 0, 1) if (dx, dy) != (0, 0)]


def padded_shape(nx, ny, nz):
    return (nx + 2 * WIDE, ny + 2 * TOP, nz)


def depth_pair(field, step):
    axis = field.ndim - 1
    depth = field.shape[axis]
    column = lax.broadcasted_iota(jnp.int32, field.shape, axis)
    ahead = jnp.where(column < depth - step, pltpu.roll(field, depth - step, axis), 0.0)
    behind = jnp.where(column >= step, pltpu.roll(field, step, axis), 0.0)
    return ahead + behind


def depth_sum(field, step):
    axis = field.ndim - 1
    depth = field.shape[axis]
    column = lax.broadcasted_iota(jnp.int32, field.shape, axis)
    ahead = pltpu.roll(field, depth - step, axis)
    behind = pltpu.roll(field, step, axis)
    return field + jnp.where((column // step) % 2 == 0, ahead, behind)


def around(ref, i, first, count, step, cut=None):
    rows = pl.ds(first, count)
    own = ref[i, rows]
    up = ref[i, pl.ds(first - 1, count)]
    down = ref[i, pl.ds(first + 1, count)]
    if cut is not None:
        up = up * cut[0]
        down = down * cut[1]
    total = ref[i - 1, rows] + ref[i + 1, rows] + (up + down)
    return own, total + depth_pair(own, step)


UNROLL = 8


def loop(low, high, body, unroll=UNROLL):
    trips = high - low
    if trips <= unroll:
        for i in range(low, high):
            body(i)
        return
    while trips % unroll:
        unroll -= 1

    def step(i, carry):
        for j in range(unroll):
            body(low + i * unroll + j)
        return carry

    lax.fori_loop(0, trips // unroll, step, 0)


X_FACES = [(-1, 0), (1, 0)]
Y_FACES = [(0, -1), (0, 1)]
CORNERS = [(-1, -1), (-1, 1), (1, -1), (1, 1)]


def halo_copies(ref, nx, ny, wide, corners, sems, base, packed, tiles):
    copies = {}
    blk, agg = lax.axis_index("blk"), lax.axis_index("agg")
    for dx, dy in SIDES:
        if corners is None and dy != 0:
            continue
        planes = wide
        if dx != 0 and dy != 0:
            if not corners:
                continue
            planes = corners
        x_from, x_to, x_count = {
            -1: (WIDE, nx + WIDE, planes),
            0: (WIDE, WIDE, nx),
            1: (nx + WIDE - planes, WIDE - planes, planes),
        }[dx]
        y_from, y_to, y_count = {
            -1: (TOP, TOP + ny, EDGE),
            0: (TOP, TOP, ny),
            1: (TOP + ny - EDGE, TOP - EDGE, EDGE),
        }[dy]
        at = base + len(copies)
        source = ref.at[pl.ds(x_from, x_count), pl.ds(y_from, y_count)]
        target = ref.at[pl.ds(x_to, x_count), pl.ds(y_to, y_count)]
        if packed is not None and dy == 0:
            source, target = (packed.at[0], packed.at[3]) if dx < 0 else (packed.at[1], packed.at[2])
        if tiles is not None and dx == 0:
            source = tiles.at[0 if dy < 0 else 1]
        copy = pltpu.make_async_remote_copy(
            src_ref=source,
            dst_ref=target,
            send_sem=sems[0].at[at],
            recv_sem=sems[1].at[at],
            device_id={"blk": blk + dx, "agg": agg + dy},
            device_id_type=pl.DeviceIdType.MESH,
        )
        copies[dx, dy] = copy
    return copies


def kernel(levels, *refs):
    refs = list(refs)
    rhs_hbm, coef_hbm, out_ref = refs[:3]
    refs = refs[3:]
    take = lambda count: [refs.pop(0) for _ in range(count)]
    vs = take(levels + 1)
    ws = take(levels + 1)
    fs = take(levels + 1)
    bs = take(levels + 1)
    cs = take(levels + 1)
    ts = take(levels)
    us = take(levels)
    ps, rhs_ref = take(2)
    faces = [None] + take(levels)
    tiles = take(1)[0]
    coef_ref = cs[0]
    send_sem, recv_sem, load_sem = take(3)

    nx, ny, nz = rhs_ref.shape
    shapes = [(nx >> k, ny >> k, nz) for k in range(levels + 1)]
    blk, agg = lax.axis_index("blk"), lax.axis_index("agg")
    n_blk, n_agg = lax.axis_size("blk"), lax.axis_size("agg")

    part = nx // 4
    loads = {}
    for at, q in enumerate((0, 3, 1, 2)):
        planes = pl.ds(q * part, part)
        loads[q] = [
            pltpu.make_async_copy(hbm.at[planes], ref.at[planes], load_sem.at[2 * at + j])
            for j, (hbm, ref) in enumerate(((coef_hbm, coef_ref), (rhs_hbm, rhs_ref)))
        ]
        for copy in loads[q]:
            copy.start()

    def inside(dx, dy):
        ok = None
        for d, at, size in ((dx, blk, n_blk), (dy, agg, n_agg)):
            if d == 0:
                continue
            this = at > 0 if d < 0 else at < size - 1
            ok = this if ok is None else jnp.logical_and(ok, this)
        return ok

    barrier = pltpu.get_barrier_semaphore()
    for dx, dy in SIDES:

        @pl.when(inside(dx, dy))
        def _():
            pl.semaphore_signal(
                barrier,
                inc=1,
                device_id={"blk": blk + dx, "agg": agg + dy},
                device_id_type=pl.DeviceIdType.MESH,
            )

    @pl.when(blk == 0)
    def _():
        for ref in vs + ws:
            ref[0:WIDE] = jnp.zeros((WIDE,) + ref.shape[1:], jnp.float32)

    @pl.when(blk == n_blk - 1)
    def _():
        for ref in vs + ws:
            high = ref.shape[0]
            ref[high - WIDE : high] = jnp.zeros((WIDE,) + ref.shape[1:], jnp.float32)

    @pl.when(agg == 0)
    def _():
        for ref in vs + ws:
            zero = jnp.zeros((ref.shape[0], EDGE, nz), jnp.float32)
            ref[:, TOP - EDGE : TOP] = zero

    @pl.when(agg == n_agg - 1)
    def _():
        for ref in vs + ws:
            high = ref.shape[1] - TOP
            zero = jnp.zeros((ref.shape[0], EDGE, nz), jnp.float32)
            ref[:, high : high + EDGE] = zero

    used = 0
    v_moves, w_moves = [], []
    for k in range(levels + 1):
        for ref, moves, planes, corners, packed, edges in (
            (vs[k], v_moves, WIDE, WIDE if k > 1 else 1, faces[k], tiles if k == 0 else None),
            (ws[k], w_moves, 1, (None, 0, 1)[min(k, 2)], None, None),
        ):
            copies = halo_copies(
                ref, *shapes[k][:2], planes, corners, (send_sem, recv_sem), used, packed, edges
            )
            moves.append(copies)
            used += len(copies)

    def pack_tiles(i):
        row = lax.broadcasted_iota(jnp.int32, (EDGE, nz), 0)
        for slot, low, kept in ((0, TOP, row < WIDE), (1, TOP + ny - EDGE, row >= EDGE - WIDE)):
            rows = pl.ds(low, EDGE)
            scale = pltpu.roll(ws[0][i + WIDE, rows], EDGE // 2, 0)
            tiles[slot, i] = jnp.where(kept, vs[0][i + WIDE, rows], scale)

    def receive_tiles():
        for dy, low in ((-1, TOP + ny), (1, TOP - EDGE)):

            @pl.when(inside(0, -dy))
            def _():
                v_moves[0][0, dy].wait_recv()
                rows = pl.ds(low, EDGE)

                def unpack(i):
                    ws[0][i + WIDE, rows] = pltpu.roll(vs[0][i + WIDE, rows], EDGE // 2, 0)

                loop(0, nx, unpack)

    def send(copies, sides):
        for dx, dy in sides:

            @pl.when(inside(dx, dy))
            def _():
                copies[dx, dy].start()

    def receive(copies, sides):
        for dx, dy in sides:

            @pl.when(inside(-dx, -dy))
            def _():
                copies[dx, dy].wait_recv()

    def first_half(k):
        column = lax.broadcasted_iota(jnp.int32, (shapes[k][1], nz), 1)
        return (column >> (k - 1)) % 2 == 0

    def pack_faces(k):
        rows = pl.ds(TOP, shapes[k][1])
        for slot, plane in ((0, WIDE), (1, shapes[k][0])):
            faces[k][slot] = jnp.where(first_half(k), vs[k][plane, rows], vs[k][plane + 1, rows])

    def receive_faces(k):
        rows, half = pl.ds(TOP, shapes[k][1]), 1 << (k - 1)
        for dx, slot, plane in ((1, 2, 0), (-1, 3, shapes[k][0] + WIDE)):

            @pl.when(inside(-dx, 0))
            def _():
                v_moves[k][dx, 0].wait_recv()
                both = faces[k][slot]
                low = first_half(k)
                vs[k][plane, rows] = jnp.where(low, both, pltpu.roll(both, half, 1))
                vs[k][plane + 1, rows] = jnp.where(low, pltpu.roll(both, nz - half, 1), both)

    own_rows = pl.ds(TOP, ny)

    def guess(i):
        scale = OMEGA / (6.0 + coef_ref[i])
        ws[0][i + WIDE, own_rows] = scale
        vs[0][i + WIDE, own_rows] = scale * rhs_ref[i]

    def guess_part(q):
        for copy in loads[q]:
            copy.wait()
        loop(q * part, (q + 1) * part, guess)

    guess_part(0)
    guess_part(3)
    count = 1
    for size, at in ((n_blk, blk), (n_agg, agg)):
        near = 1 + (at > 0).astype(jnp.int32) + (at < size - 1).astype(jnp.int32)
        count = count * near
    pl.semaphore_wait(barrier, count - 1)
    send(v_moves[0], X_FACES)
    send(w_moves[0], X_FACES)
    send(v_moves[0], CORNERS)
    guess_part(1)
    guess_part(2)
    loop(0, nx, pack_tiles)
    send(v_moves[0], Y_FACES)

    def coarsened(source, k, i):
        rows = shapes[k][1]
        held = ts[k - 1]
        held[i] = source
        pair = held[i, pl.ds(0, rows, stride=2)] + held[i, pl.ds(1, rows, stride=2)]
        return 0.5 * depth_sum(pair, 1 << (k - 1))

    for k in range(1, levels + 1):

        def scales(i, k=k):
            coef = coarsened(cs[k - 1][2 * i] + cs[k - 1][2 * i + 1], k, i)
            cs[k][i] = coef
            ws[k][i + WIDE, pl.ds(TOP, shapes[k][1])] = OMEGA / (6.0 + coef)

        loop(0, shapes[k][0], scales)

    fine_rows = pl.ds(TOP - EDGE, ny + 2 * EDGE)

    def smooth_fine(i):
        own, total = around(vs[0], i, TOP - EDGE, ny + 2 * EDGE, 1)
        ps[i, fine_rows] = 1.2 * own + ws[0][i, fine_rows] * total
        return total[EDGE : EDGE + ny]

    def smooth_own(i):
        total = smooth_fine(i + WIDE)
        bs[0][i] = 0.04 * rhs_ref[i] - OMEGA * total

    def fine_residual(i):
        own, total = around(ps, i + WIDE, TOP, ny, 1)
        at = i + WIDE
        fs[0][at, own_rows] = 0.2 * own + (vs[0][at, own_rows] + ws[0][at, own_rows] * total)
        return bs[0][i] + total

    def cuts(k, first, rows):
        span = 1 << k
        low = (agg % span != 0).astype(jnp.float32)
        high = ((agg + 1) % span != 0).astype(jnp.float32)
        row = first + lax.broadcasted_iota(jnp.int32, (rows, nz), 0)
        end = TOP + shapes[k][1]
        up = jnp.where(row == TOP, low, jnp.where(row == end, high, 1.0))
        down = jnp.where(row == TOP - 1, low, jnp.where(row == end - 1, high, 1.0))
        return up, down

    def relax(k):
        ky = shapes[k][1]
        cut = cuts(k, TOP - EDGE, ky + 2 * EDGE)
        rows = pl.ds(TOP - EDGE, ky + 2 * EDGE)

        def body(i):
            own, total = around(vs[k], i, TOP - EDGE, ky + 2 * EDGE, 1 << k, cut)
            result = 1.2 * own + ws[k][i, rows] * total
            if k == levels:
                spread(k, i, result)
            else:
                fs[k][i, rows] = result

        loop(1, shapes[k][0] + WIDE + 1, body)

    def spread(k, i, error):
        count = shapes[k][1] + 2 * EDGE
        us[k - 1][i, pl.ds(0, count, stride=2)] = error
        us[k - 1][i, pl.ds(1, count, stride=2)] = error

    for k in range(1, levels + 1):
        kx, ky, _ = shapes[k]
        if k == 1:
            residual = fine_residual
        else:
            cut = cuts(k - 1, TOP, shapes[k - 1][1])

            def residual(i, k=k, cut=cut):
                _, total = around(
                    vs[k - 1], i + WIDE, TOP, shapes[k - 1][1], 1 << (k - 1), cut
                )
                return 0.2 * bs[k - 1][i] + total

        def descend(i, k=k, residual=residual):
            source = coarsened(residual(2 * i) + residual(2 * i + 1), k, i)
            bs[k][i] = source
            rows = pl.ds(TOP, shapes[k][1])
            vs[k][i + WIDE, rows] = ws[k][i + WIDE, rows] * source

        if k > 1:
            receive(v_moves[k - 1], Y_FACES)
        else:
            receive_tiles()
            loop(1, nx - 1, smooth_own)
        loop(1, kx - 1, descend)
        if k > 1:
            receive_faces(k - 1)
        else:
            for moves in w_moves[1:]:
                send(moves, list(moves))
            receive(v_moves[0], X_FACES + CORNERS)
            receive(w_moves[0], X_FACES)
            smooth_fine(WIDE - 1)
            smooth_own(0)
            smooth_own(nx - 1)
            smooth_fine(nx + WIDE)
        descend(0)
        descend(kx - 1)
        pack_faces(k)
        send(v_moves[k], X_FACES + Y_FACES + CORNERS)
        if k > 1:
            receive(v_moves[k - 1], CORNERS)
            receive(w_moves[k - 1], list(w_moves[k - 1]))
            relax(k - 1)

    def drain(moves):
        for copies in moves:
            for (dx, dy), copy in copies.items():

                @pl.when(inside(dx, dy))
                def _():
                    copy.wait_send()

    drain(v_moves[:levels] + w_moves)
    receive(w_moves[levels], list(w_moves[levels]))
    receive(v_moves[levels], Y_FACES + CORNERS)
    receive_faces(levels)
    relax(levels)

    for k in range(levels - 1, -1, -1):
        kx, ky, _ = shapes[k]
        over = EDGE if k else 0
        count = ky + 2 * over
        rows = pl.ds(TOP - over, count)
        cut = cuts(k, TOP - over, count) if k else None

        def correct(i, k=k, count=count, rows=rows, cut=cut, over=over):
            coarse = us[k]
            own = coarse[i, rows]
            up = coarse[i, pl.ds(TOP - over - 1, count)]
            down = coarse[i, pl.ds(TOP - over + 1, count)]
            if cut is not None:
                up = up * cut[0]
                down = down * cut[1]
            inner = own + (up + down) + depth_pair(own, 1 << k)
            for j in range(2):
                at = 2 * (i - 1) + j
                total = inner + coarse[i - 1 + 2 * j, rows]
                result = fs[k][at, rows] + (0.2 * own + ws[k][at, rows] * total)
                if k == 0:
                    out_ref[at - WIDE] = result
                else:
                    spread(k, at, result)

        if k == 0:
            loop(WIDE, kx // 2 + WIDE, correct)
        else:
            loop(1, kx // 2 + WIDE + 1, correct)

    drain(v_moves[levels:])


def shards(right_side, coefficient):
    levels = lax.axis_size("agg").bit_length() - 1
    nx, ny, nz = right_side.shape
    shapes = [(nx >> k, ny >> k, nz) for k in range(levels + 1)]
    vmem = lambda shape: pltpu.VMEM(shape, jnp.float32)
    padded = [vmem(padded_shape(*shape)) for shape in shapes]
    plain = [vmem(shape) for shape in shapes]
    halves = [vmem((shapes[k + 1][0], shapes[k][1], nz)) for k in range(levels)]
    spreads = [
        vmem((shapes[k + 1][0] + 2 * WIDE, shapes[k][1] + 2 * TOP, nz)) for k in range(levels)
    ]
    faces = [vmem((4,) + shape[1:]) for shape in shapes[1:]]
    tiles = vmem((2, nx, EDGE, nz))
    moves = 16 * (levels + 1)
    sems = [pltpu.SemaphoreType.DMA((moves,))] * 2 + [pltpu.SemaphoreType.DMA((8,))]
    cells = nx * ny * nz
    return pl.pallas_call(
        functools.partial(kernel, levels),
        out_shape=pltpu.VMEM(right_side.shape, right_side.dtype),
        in_specs=[pl.BlockSpec(memory_space=pltpu.HBM)] * 2,
        out_specs=pl.BlockSpec(memory_space=pltpu.VMEM),
        scratch_shapes=padded * 3 + plain * 2 + halves + spreads + [padded[0], plain[0]] + faces + [tiles] + sems,
        compiler_params=pltpu.CompilerParams(
            collective_id=0, has_side_effects=True, vmem_limit_bytes=58 * 2**20
        ),
        cost_estimate=pl.CostEstimate(
            flops=60 * cells, bytes_accessed=12 * cells, transcendentals=0
        ),
        name="vcycle",
    )(right_side, coefficient)


def solution(mesh):
    placed = (P("blk", "agg", None), P("blk", "agg", None))
    return jax.shard_map(
        shards, mesh=mesh, in_specs=placed, out_specs=P("blk", "agg", None), check_vma=False
    )
```
